256 devices in a mesh: pipe: 16 (over x_lo, y, core), expert: 8 (over z), dp: 2 (over x_hi).
Axes of the slice: x: 4 (x_hi: 2, x_lo: 2; x = x_hi * 2 + x_lo), y: 4, z: 8, core: 2. Of those that a mesh axis runs over, the one named last changes fastest.
Arguments:
- fwd_in: bfloat16 [16, 2048, 3584], P('pipe', ('expert', 'dp')), may hold values from -6 to 6
- fwd_ids: int32 [16, 2048, 1], P('pipe', ('expert', 'dp')), may hold values from 0 to 3; in each aligned block of 128 rows (0 to 127, 128 to 255, ..., all dimensions but the last counted through in order) at most 40 rows name the same one
- fwd_gates: float32 [16, 2048, 1], P('pipe', ('expert', 'dp')), may hold values from 0.2 to 1
- bwd_in: bfloat16 [16, 2048, 3584], P('pipe', ('expert', 'dp')), may hold values from -6 to 6
- bwd_grad: bfloat16 [16, 2048, 3584], P('pipe', ('expert', 'dp')), may hold values from -6 to 6
- bwd_ids: int32 [16, 2048, 1], P('pipe', ('expert', 'dp')), may hold values from 0 to 3; in each aligned block of 128 rows (0 to 127, 128 to 255, ..., all dimensions but the last counted through in order) at most 40 rows name the same one
- bwd_gates: float32 [16, 2048, 1], P('pipe', ('expert', 'dp')), may hold values from 0.2 to 1
- gate_w: bfloat16 [16, 3584, 4096], P('pipe', 'dp', 'expert'), may hold values from -0.09375 to 0.09375
- up_w: bfloat16 [16, 3584, 4096], P('pipe', 'dp', 'expert'), may hold values from -0.09375 to 0.09375
- down_w: bfloat16 [16, 3584, 4096], P('pipe', 'dp', 'expert'), may hold values from -0.1875 to 0.1875
Outputs:
- fwd_next: bfloat16 [16, 2048, 3584], P('pipe', ('expert', 'dp'))
- bwd_next: bfloat16 [16, 2048, 3584], P('pipe', ('expert', 'dp'))
- gate_grad: bfloat16 [16, 3584, 4096], P('pipe', 'dp', 'expert')
The draws below stay inside these ranges and needn't reach their ends.
Inputs may be any that keep to these rules, and one draw needn't show every extreme that they name: `fwd_ids`: at every section the 128 tokens of one routing block (aligned blocks of rows) name any expert at most 40 times, a bound that some block reaches; each token names exactly 1 expert. `bwd_ids`: as for fwd_ids.
All inputs are finite; a program needn't handle non-finite values.
Results may differ from the reference program's by a relative error of at most 0.01.
Values may be sent and summed in bfloat16 or wider, within the bound.
A program may use at most 128 MiB of HBM per device.

```python
import math
import jax
import jax.numpy as jnp
import numpy as np
from jax import lax

D = 3584
F = 1024
TOPK = 1
SPLIT = 2
SECTIONS = 16
EXPERTS = 4
ROWS = 128
TOKENS_MB = 2048
CAP = 40
N_DP = 2


def shard_levels(stream_key, dims, split, least, largest):
    factor_of = 1.0
    for position, parts in split:
        steps = jax.random.uniform(jax.random.fold_in(jax.random.fold_in(stream_key, 6), position), (parts,), jnp.float32, least / len(split), largest / len(split))
        factor_of = factor_of * jnp.repeat(jnp.exp(steps), dims[position] // parts).reshape((-1,) + (1,) * (len(dims) - 1 - position))
    return factor_of


def assign_block(own_key, own, number, rows, amount, top, bound, skew):
    ranking = jax.random.permutation(own_key, amount)
    crowded, usual = load_shares(amount, rows * top, bound, skew, True), load_shares(amount, rows * top, bound, skew, False)
    places = jnp.arange(amount)

    def named(sizes, turn):
        used = int((sizes > 0).sum())
        fixed = max(1, used // 4)
        moved = fixed + (places - fixed + turn * (used - fixed)) % max(1, amount - fixed)
        return jnp.zeros((amount,), jnp.int32).at[ranking[jnp.where(places < fixed, places, moved)]].set(jnp.asarray(sizes, jnp.int32))

    sizes = jnp.where(number % 4 == 0, named(crowded, number // 4), named(usual, number - number // 4 - 1))
    mixed = jax.random.permutation(jax.random.fold_in(own, 3), amount)
    source_of, taker = mixed[0:amount // 2 * 2:2], mixed[1:amount // 2 * 2:2]
    room = jnp.minimum(sizes[source_of] - 1, bound - sizes[taker]) // 2
    room = jnp.where((source_of == ranking[0]) | (taker == ranking[0]) | (sizes[taker] == 0), 0, jnp.maximum(room, 0))
    moved = jax.random.randint(jax.random.fold_in(own, 4), (amount // 2,), 0, 1 << 20) % (room + 1)
    sizes = sizes.at[source_of].add(-moved).at[taker].add(moved)
    members = jnp.searchsorted(jnp.cumsum(sizes), jnp.arange(rows * top), side="right").astype(jnp.int32)
    table = members.reshape(top, rows).T
    table = table[jax.random.permutation(jax.random.fold_in(own, 1), rows)]
    turn = jax.random.randint(jax.random.fold_in(own, 2), (rows, 1), 0, top)
    return jnp.take_along_axis(table, (jnp.arange(top)[None, :] + turn) % top, axis=1)


def load_shares(number_of, total, reach, slope, full):
    loads = [(1 << 20) // math.isqrt(rank ** slope) + 1 for rank in range(1, number_of + 1)]
    largest = reach if full else min(reach, max(-(-total // number_of), total * loads[0] // sum(loads)))
    least = 1 if total - largest >= number_of - 1 else 0
    holding, spare = [largest] + [least] * (number_of - 1), total - largest - least * (number_of - 1)
    while spare > 0:
        candidates = [i for i in range(1, number_of) if holding[i] < largest] or [i for i in range(1, number_of) if holding[i] < reach]
        whole, left = sum([loads[i] for i in candidates]), spare
        for i in candidates:
            addition = min(reach - holding[i], max(1, left * loads[i] // whole), spare)
            holding[i] = holding[i] + addition
            spare = spare - addition
    return np.array(holding)


def scatter_about(stream_key, dims, width, bound, pieces=(), kind=jnp.bfloat16):
    factor_of = shard_levels(stream_key, dims, pieces, -0.22, 0.18) if pieces else 1.0
    result = jax.random.normal(stream_key, dims, jnp.float32) * width * factor_of
    return jnp.minimum(jnp.maximum(result, -bound), bound).astype(kind)


def setup_inputs(seed: int = 0) -> dict:
    key_list = jax.random.split(jax.random.key(seed), 11)
    fwd_in = scatter_about(key_list[0], (SECTIONS, TOKENS_MB, D), 1.0, 6.0, ((0, 16), (1, 16)))
    fwd_ids_keys = jax.random.split(jax.random.fold_in(key_list[1], 1), SECTIONS * TOKENS_MB // ROWS)
    fwd_ids_turns = jax.random.permutation(jax.random.fold_in(key_list[1], 3), SECTIONS * TOKENS_MB // ROWS)
    fwd_ids = jax.vmap(lambda own, number: assign_block(jax.random.fold_in(key_list[1], 2), own, number, ROWS, EXPERTS, TOPK, CAP, 2))(fwd_ids_keys, fwd_ids_turns).reshape((SECTIONS, TOKENS_MB, TOPK))
    fwd_gates = jnp.clip(0.2 + 0.8 * jax.random.uniform(key_list[2], (SECTIONS, TOKENS_MB, TOPK), jnp.float32) ** shard_levels(key_list[2], (SECTIONS, TOKENS_MB, TOPK), ((0, 16), (1, 16)), -0.2, 0.2), 0.2, 1.0)
    bwd_in = scatter_about(key_list[3], (SECTIONS, TOKENS_MB, D), 1.0, 6.0, ((0, 16), (1, 16)))
    bwd_grad = scatter_about(key_list[4], (SECTIONS, TOKENS_MB, D), 1.0, 6.0, ((0, 16), (1, 16)))
    bwd_ids_keys = jax.random.split(jax.random.fold_in(key_list[5], 1), SECTIONS * TOKENS_MB // ROWS)
    bwd_ids_turns = jax.random.permutation(jax.random.fold_in(key_list[5], 3), SECTIONS * TOKENS_MB // ROWS)
    bwd_ids = jax.vmap(lambda own, number: assign_block(jax.random.fold_in(key_list[5], 2), own, number, ROWS, EXPERTS, TOPK, CAP, 2))(bwd_ids_keys, bwd_ids_turns).reshape((SECTIONS, TOKENS_MB, TOPK))
    bwd_gates = jnp.clip(0.2 + 0.8 * jax.random.uniform(key_list[6], (SECTIONS, TOKENS_MB, TOPK), jnp.float32) ** shard_levels(key_list[6], (SECTIONS, TOKENS_MB, TOPK), ((0, 16), (1, 16)), -0.2, 0.2), 0.2, 1.0)
    gate_w = scatter_about(key_list[7], (SECTIONS, D, EXPERTS * F), D ** -0.5, 0.09375, ((0, 16), (1, 2), (2, 8)))
    up_w = scatter_about(key_list[8], (SECTIONS, D, EXPERTS * F), D ** -0.5, 0.09375, ((0, 16), (1, 2), (2, 8)))
    down_w = scatter_about(key_list[9], (SECTIONS, D, EXPERTS * F), F ** -0.5, 0.1875, ((0, 16), (1, 2), (2, 8)))
    return {"fwd_in": fwd_in, "fwd_ids": fwd_ids, "fwd_gates": fwd_gates, "bwd_in": bwd_in, "bwd_grad": bwd_grad, "bwd_ids": bwd_ids, "bwd_gates": bwd_gates, "gate_w": gate_w, "up_w": up_w, "down_w": down_w}


def assign(ids):
    blocks = ids.shape[0] // ROWS
    flat = ids.reshape(blocks, ROWS * TOPK)
    onehot = (flat[:, :, None] == jnp.arange(EXPERTS, dtype=jnp.int32)[None, None, :]).astype(jnp.int32)
    ranked = jnp.sum(onehot * (jnp.cumsum(onehot, axis=1) - 1), axis=2)
    block_no = jnp.arange(blocks, dtype=jnp.int32)[:, None]
    return (flat * (blocks * CAP) + block_no * CAP + ranked).reshape(-1).astype(jnp.int32), blocks


def dispatch(rows, index, blocks):
    empty = jnp.zeros((EXPERTS * blocks * CAP, D), rows.dtype)
    return empty.at[index].set(rows).reshape(EXPERTS, blocks * CAP, D)


def collect(output, index, gates, base):
    picked = output.reshape(-1, D)[index].reshape(gates.shape[0], TOPK, D)
    total = base.astype(jnp.float32) + jnp.sum(gates[:, :, None] * picked, axis=1)
    return total.astype(jnp.bfloat16)


def per_expert(weight):
    return weight.reshape(D, EXPERTS, F).transpose(1, 0, 2).astype(jnp.float32)


def halves(pairs):
    total = None
    for left, weight in pairs:
        left_h = left.reshape(left.shape[0], left.shape[1], SPLIT, F // SPLIT)
        weight_h = weight.reshape(weight.shape[0], D, SPLIT, F // SPLIT)
        term = jnp.einsum('erhf,edhf->herd', left_h, weight_h)
        total = term if total is None else total + term
    rounded = lax.optimization_barrier(total.astype(jnp.bfloat16))
    return jnp.sum(rounded.astype(jnp.float32), axis=0)


def grad_sum(rows, inner, blocks):
    rows_p = rows.reshape(EXPERTS, blocks // N_DP, N_DP, CAP, rows.shape[2])
    inner_p = inner.reshape(EXPERTS, blocks // N_DP, N_DP, CAP, F)
    part = jnp.einsum('ejpcd,ejpcf->pedf', rows_p, inner_p)
    rounded = lax.optimization_barrier(part.astype(jnp.bfloat16))
    total = jnp.sum(rounded.astype(jnp.float32), axis=0).astype(jnp.bfloat16)
    return total.transpose(1, 0, 2).reshape(D, EXPERTS * F)


def section(items):
    f_in, f_ids, f_gates, b_in, b_grad, b_ids, b_gates, w_gate, w_up, w_down = items
    w_gate32 = per_expert(w_gate)
    w_up32 = per_expert(w_up)
    w_down32 = per_expert(w_down)
    f_index, blocks = assign(f_ids)
    f_buf = dispatch(jnp.repeat(f_in, TOPK, axis=0), f_index, blocks).astype(jnp.float32)
    gate_pre = jnp.einsum('erd,edf->erf', f_buf, w_gate32)
    up_pre = jnp.einsum('erd,edf->erf', f_buf, w_up32)
    hidden = (jax.nn.silu(gate_pre) * up_pre).astype(jnp.bfloat16)
    output = halves([(hidden.astype(jnp.float32), w_down32)])
    layer_out = collect(output, f_index, f_gates, f_in)

    b_index, blocks = assign(b_ids)
    scaled = (b_gates[:, :, None] * b_grad[:, None, :].astype(jnp.float32)).astype(jnp.bfloat16).reshape(-1, D)
    x_buf = dispatch(jnp.repeat(b_in, TOPK, axis=0), b_index, blocks).astype(jnp.float32)
    z_buf = dispatch(scaled, b_index, blocks).astype(jnp.float32)
    gate_pre = jnp.einsum('erd,edf->erf', x_buf, w_gate32)
    up_pre = jnp.einsum('erd,edf->erf', x_buf, w_up32)
    sigma = jax.nn.sigmoid(gate_pre)
    active = gate_pre * sigma
    d_hidden = jnp.einsum('erd,edf->erf', z_buf, w_down32)
    d_gate = (d_hidden * up_pre * sigma * (1.0 + gate_pre * (1.0 - sigma))).astype(jnp.bfloat16)
    d_up = (d_hidden * active).astype(jnp.bfloat16)
    back = halves([(d_gate.astype(jnp.float32), w_gate32), (d_up.astype(jnp.float32), w_up32)])
    input_grad = collect(back, b_index, jnp.ones_like(b_gates), b_grad)
    gate_grad = grad_sum(x_buf, d_gate.astype(jnp.float32), blocks)
    return layer_out, input_grad, gate_grad


def reference(fwd_in, fwd_ids, fwd_gates, bwd_in, bwd_grad, bwd_ids, bwd_gates, gate_w, up_w, down_w):
    layer_out, input_grad, gate_grad = lax.map(
        section, (fwd_in, fwd_ids, fwd_gates, bwd_in, bwd_grad, bwd_ids, bwd_gates, gate_w, up_w, down_w))
    fwd_next = jnp.roll(layer_out, 1, axis=0)
    bwd_next = jnp.roll(input_grad, -1, axis=0)
    return fwd_next, bwd_next, gate_grad
```

```python
import functools

import jax
import jax.numpy as jnp
from jax import lax
from jax.experimental import pallas as pl
from jax.experimental.pallas import tpu as pltpu
from jax.sharding import PartitionSpec as P

MESH = pl.DeviceIdType.MESH
BF16, F32 = jnp.bfloat16, jnp.float32
X, Z, FW = 0, 1, 2
BACK, OUT = 0, 1
STEP = 256
ROLES = 96

SEND_GROUPS = {X: ((0, 2), (2, 7)), Z: ((0, 7),), FW: ((0, 7),)}
BACK_GROUPS = {BACK: ((0, 7),), OUT: ((0, 4), (4, 7))}


def kernel(
    sections, holders, cap,
    fwd_in, fwd_ids, fwd_gates, bwd_in, bwd_grad, bwd_ids, bwd_gates, gate_w, up_w, down_w,
    fwd_next, bwd_next, gate_grad,
    raw, wts, packed, recv, sel, slots, gts, pout, pin, acc, hid, part, part_in, ret, fin, grad,
    local_sem, send_sem, recv_sem,
):
    rows = fwd_in.shape[1]
    half, units = gate_w.shape[1], gate_w.shape[2]
    unit = 2 * cap
    quad = 4 * unit
    s, z, q = lax.axis_index("pipe"), lax.axis_index("expert"), lax.axis_index("dp")
    odd = z % 2
    o = 2 * odd - 1

    def at_z(offset):
        return (s, (z + offset * o + holders) % holders, q)

    twin = (s, z, 1 - q)
    mate = at_z(-1)
    section_after, section_before = (s + 1) % sections, (s + sections - 1) % sections
    peers = [twin, mate, at_z(1), at_z(2), at_z(-2), at_z(3)]
    peers += [(t, z, d) for t in (section_after, section_before) for d in (q, 1 - q)]

    roles = []

    def send(src, dst, device):
        i = len(roles)
        copy = pltpu.make_async_remote_copy(
            src_ref=src, dst_ref=dst, send_sem=send_sem.at[i], recv_sem=recv_sem.at[i],
            device_id=device, device_id_type=MESH,
        )
        roles.append(copy)
        copy.start()
        return copy

    def block(j):
        return pl.ds(j * unit, unit)

    def cols(group):
        return pl.ds(group[0] * STEP, (group[1] - group[0]) * STEP)

    mine = pl.ds(pl.multiple_of(q * rows, rows), rows)
    own_half = pl.ds(pl.multiple_of(q * half, half), half)
    own_rows = pl.ds(pl.multiple_of(q * quad, quad), quad)
    other_rows = pl.ds(pl.multiple_of((1 - q) * quad, quad), quad)
    tokens = {X: bwd_in, Z: bwd_grad, FW: fwd_in}

    loads = {}
    for a in (X, Z, FW):
        loads[a] = pltpu.make_async_copy(
            tokens[a].at[0, :, own_half], raw.at[a, mine, :], local_sem.at[a]
        )
        loads[a].start()
    weight_loads = []
    for i, w in enumerate((gate_w, up_w, down_w)):
        weight_loads.append(pltpu.make_async_copy(w.at[0], wts.at[i], local_sem.at[3 + i]))
        weight_loads[-1].start()

    before = lax.broadcasted_iota(jnp.int32, (rows, rows), 0) < lax.broadcasted_iota(
        jnp.int32, (rows, rows), 1
    )
    pair = (z // 2).astype(F32)
    step_up = (2 - odd).astype(F32)
    step_down = (1 + odd).astype(F32)
    for i, (ids, gates) in enumerate(((bwd_ids, bwd_gates), (fwd_ids, fwd_gates))):
        down = jnp.broadcast_to(ids[0].astype(F32), (rows, rows))
        across = down.T
        same = jnp.where((down == across) & before, 1.0, 0.0)
        rank = jnp.sum(same, axis=0, keepdims=True)
        delta = across[0:1, :] - pair
        delta = jnp.where(delta < 0.0, delta + 4.0, delta)
        place = jnp.where(
            delta == 0.0, 0.0,
            jnp.where(delta == 2.0, 3.0, jnp.where(delta == 1.0, step_up, step_down)),
        )
        slot = place * unit + q.astype(F32) * cap + rank
        slots[q, pl.ds(8 * i, 8), :] = jnp.broadcast_to(slot, (8, rows))
        gts[q, i] = jnp.broadcast_to(gates[0], (rows, rows))

    barrier = pltpu.get_barrier_semaphore()
    for peer in peers:
        pl.semaphore_signal(barrier, inc=1, device_id=peer, device_id_type=MESH)
    pl.semaphore_wait(barrier, len(peers))

    meta = [send(slots.at[q], slots.at[q], twin), send(gts.at[q], gts.at[q], twin)]
    cross = {}
    for a in (X, Z, FW):
        for group in SEND_GROUPS[a]:
            width = (group[1] - group[0]) * STEP
            start = pl.multiple_of((1 - q) * half + group[0] * STEP, STEP)
            cross[a, group] = send(
                tokens[a].at[0, :, pl.ds(start, width)], raw.at[a, mine, cols(group)], twin
            )
    for copy in meta:
        copy.wait_recv()
    for i in range(2):
        for b in range(2):
            slot = slots[b, 8 * i : 8 * i + 1, :]
            index = lax.broadcasted_iota(jnp.int32, (quad, rows), 0).astype(F32)
            sel[i, :, b * rows : (b + 1) * rows] = jnp.where(index == slot, 1.0, 0.0).astype(BF16)

    direct, passed = {}, {}

    def pack(a):
        for group in SEND_GROUPS[a]:
            if group[0] == 0:
                loads[a].wait()
            cross[a, group].wait_recv()

            @pl.loop(group[0], group[1])
            def _(c):
                at = pl.ds(pl.multiple_of(c * STEP, STEP), STEP)
                block_in = raw[a, :, at]
                if a == Z:
                    gate = jnp.concatenate([gts[0, 0][:, 0:1], gts[1, 0][:, 0:1]], axis=0)
                    block_in = (gate * block_in.astype(F32)).astype(BF16)
                placed = jnp.dot(
                    sel[0 if a != FW else 1], block_in, preferred_element_type=F32
                ).astype(BF16)
                recv[a, 0:unit, at] = placed[0:unit]
                packed[a, :, at] = placed[unit:]

            w = cols(group)
            for j, offset in ((3, 3), (2, -2), (1, 1)):
                direct[a, group, j] = send(
                    packed.at[a, pl.ds((j - 1) * unit, unit), w], recv.at[a, block(j), w],
                    at_z(offset),
                )
            direct[a, group, 0] = send(recv.at[a, block(0), w], recv.at[a, block(7), w], mate)

    def pass_on(a):
        for group in SEND_GROUPS[a]:
            w = cols(group)
            for j in (1, 2, 3):
                direct[a, group, j].wait_recv()
                passed[a, group, j] = send(
                    recv.at[a, block(j), w], recv.at[a, block(7 - j), w], mate
                )

    def arrived(a):
        for group in SEND_GROUPS[a]:
            direct[a, group, 0].wait_recv()
            for j in (1, 2, 3):
                passed[a, group, j].wait_recv()

    def project(a, w, i):
        pout[i] = jnp.dot(recv[a, other_rows, :], wts[w], preferred_element_type=F32).astype(BF16)
        return send(pout.at[i], pin.at[i], twin)

    def project_own(a, w, i):
        acc[i] = jnp.dot(recv[a, own_rows, :], wts[w], preferred_element_type=F32)

    pack(X)
    pack(Z)
    pass_on(X)
    pack(FW)
    arrived(X)
    for load in weight_loads:
        load.wait()
    sums = {i: project(X, i, i) for i in (0, 1)}
    for i in (0, 1):
        project_own(X, i, i)
    pass_on(Z)
    arrived(Z)
    sums[2] = project(Z, 2, 2)
    project_own(Z, 2, 2)
    pass_on(FW)
    for i in range(3):
        sums[i].wait_recv()

    tile = 32

    @pl.loop(0, quad // tile)
    def _(r):
        at = pl.ds(pl.multiple_of(r * tile, tile), tile)
        to = pl.ds(pl.multiple_of(q * quad + r * tile, tile), tile)
        gate = acc[0, at, :] + pin[0, at, :].astype(F32)
        up = acc[1, at, :] + pin[1, at, :].astype(F32)
        dh = acc[2, at, :] + pin[2, at, :].astype(F32)
        sigma = jax.nn.sigmoid(gate)
        hid[0, to, :] = (dh * up * sigma * (1.0 + gate * (1.0 - sigma))).astype(BF16)
        hid[1, to, :] = (dh * (gate * sigma)).astype(BF16)

    shared = {i: send(hid.at[i, own_rows, :], hid.at[i, own_rows, :], twin) for i in (0, 1)}

    def expand(r, group, terms, lo):
        @pl.loop(group[0], group[1])
        def _(c):
            at = pl.ds(pl.multiple_of(c * STEP, STEP), STEP)
            total = None
            for i, w in terms:
                term = lax.dot_general(
                    hid[i, lo : lo + quad, :], wts[w, at, :], (((1,), (1,)), ((), ())),
                    preferred_element_type=F32,
                )
                total = term if total is None else total + term
            part[r, lo : lo + quad, at] = total.astype(BF16)

    halves, returned = {}, {}

    def give(r, terms):
        for group in BACK_GROUPS[r]:
            expand(r, group, terms, quad)
            w = cols(group)
            for j in (4, 5, 6, 7):
                halves[r, group, j] = send(
                    part.at[r, block(j), w], part_in.at[r, block(7 - j), w], mate
                )
        for group in BACK_GROUPS[r]:
            expand(r, group, terms, 0)

    def merge(r):
        for group in BACK_GROUPS[r]:
            w = cols(group)
            for j, offset in ((3, 3), (2, 2), (1, 1), (0, 0)):
                halves[r, group, 7 - j].wait_recv()

                @pl.loop(group[0], group[1])
                def _(c):
                    at = pl.ds(pl.multiple_of(c * STEP, STEP), STEP)
                    total = (
                        part[r, block(j), at].astype(F32) + part_in[r, block(j), at].astype(F32)
                    ).astype(BF16)
                    if j == 0:
                        ret[r, block(0), at] = total
                    else:
                        part[r, block(j), at] = total

                if j:
                    returned[r, group, j] = send(
                        part.at[r, block(j), w], ret.at[r, block(j), w], at_z(offset)
                    )

    last = []

    def finish(r):
        a, i, section, target = (
            (Z, 0, section_before, bwd_next) if r == BACK else (FW, 1, section_after, fwd_next)
        )
        for group in BACK_GROUPS[r]:
            for j in (1, 2, 3):
                returned[r, group, j].wait_recv()

            @pl.loop(group[0], group[1])
            def _(c):
                at = pl.ds(pl.multiple_of(c * STEP, STEP), STEP)
                picked = lax.dot_general(
                    sel[i], ret[r, :, at], (((0,), (0,)), ((), ())), preferred_element_type=F32
                )
                if r == OUT:
                    gate = jnp.concatenate([gts[0, 1][:, 0:1], gts[1, 1][:, 0:1]], axis=0)
                    picked = gate * picked
                fin[r, :, at] = (raw[a, :, at].astype(F32) + picked).astype(BF16)

            width = (group[1] - group[0]) * STEP
            start = pl.multiple_of(q * half + group[0] * STEP, STEP)
            for device in (1 - q, q):
                from_rows = pl.ds(pl.multiple_of(device * rows, rows), rows)
                last.append(
                    send(
                        fin.at[r, from_rows, cols(group)],
                        target.at[0, :, pl.ds(start, width)],
                        (section, z, device),
                    )
                )

    for i in (0, 1):
        shared[i].wait_recv()
    give(BACK, ((0, 0), (1, 1)))

    arrived(FW)
    for i in (0, 1):
        sums[3 + i] = project(FW, i, 3 + i)
    merge(BACK)
    for i in (0, 1):
        project_own(FW, i, i)
    for i in (3, 4):
        sums[i].wait_recv()

    @pl.loop(0, quad // tile)
    def _(r):
        at = pl.ds(pl.multiple_of(r * tile, tile), tile)
        to = pl.ds(pl.multiple_of(q * quad + r * tile, tile), tile)
        gate = acc[0, at, :] + pin[3, at, :].astype(F32)
        up = acc[1, at, :] + pin[4, at, :].astype(F32)
        hid[2, to, :] = (gate * jax.nn.sigmoid(gate) * up).astype(BF16)

    shared[2] = send(hid.at[2, own_rows, :], hid.at[2, own_rows, :], twin)

    @pl.loop(0, half // STEP)
    def _(c):
        at = pl.ds(pl.multiple_of(c * STEP, STEP), STEP)
        grad[at, :] = lax.dot_general(
            recv[X, :, at], hid[0], (((0,), (0,)), ((), ())), preferred_element_type=F32
        ).astype(BF16)

    store = pltpu.make_async_copy(grad, gate_grad.at[0], local_sem.at[6])
    store.start()
    shared[2].wait_recv()
    give(OUT, ((2, 2),))
    merge(OUT)
    finish(BACK)
    finish(OUT)
    for copy in last:
        copy.wait_recv()
    for copy in roles:
        copy.wait_send()
    store.wait()


def per_device(
    fwd_in, fwd_ids, fwd_gates, bwd_in, bwd_grad, bwd_ids, bwd_gates, gate_w, up_w, down_w
):
    sections, holders = lax.axis_size("pipe"), lax.axis_size("expert")
    rows, width = fwd_in.shape[1], fwd_in.shape[2]
    half, units = gate_w.shape[1], gate_w.shape[2]
    experts = holders // 2
    cap = rows * 5 // (4 * experts)
    quad = 8 * cap
    hbm = pl.BlockSpec(memory_space=pl.ANY)
    vmem = pl.BlockSpec(memory_space=pltpu.VMEM)
    return pl.pallas_call(
        functools.partial(kernel, sections, holders, cap),
        out_shape=(
            jax.ShapeDtypeStruct(fwd_in.shape, BF16),
            jax.ShapeDtypeStruct(bwd_in.shape, BF16),
            jax.ShapeDtypeStruct(gate_w.shape, BF16),
        ),
        in_specs=[hbm, vmem, vmem, hbm, hbm, vmem, vmem, hbm, hbm, hbm],
        out_specs=(hbm, hbm, hbm),
        scratch_shapes=[
            pltpu.VMEM((3, 2 * rows, half), BF16),
            pltpu.VMEM((3, half, units), BF16),
            pltpu.VMEM((3, 6 * cap, half), BF16),
            pltpu.VMEM((3, 2 * quad, half), BF16),
            pltpu.VMEM((2, quad, 2 * rows), BF16),
            pltpu.VMEM((2, 16, rows), F32),
            pltpu.VMEM((2, 2, rows, rows), F32),
            pltpu.VMEM((5, quad, units), BF16),
            pltpu.VMEM((5, quad, units), BF16),
            pltpu.VMEM((3, quad, units), F32),
            pltpu.VMEM((3, 2 * quad, units), BF16),
            pltpu.VMEM((2, 2 * quad, half), BF16),
            pltpu.VMEM((2, quad, half), BF16),
            pltpu.VMEM((2, quad, half), BF16),
            pltpu.VMEM((2, 2 * rows, half), BF16),
            pltpu.VMEM((half, units), BF16),
            pltpu.SemaphoreType.DMA((7,)),
            pltpu.SemaphoreType.DMA((ROLES,)),
            pltpu.SemaphoreType.DMA((ROLES,)),
        ],
        compiler_params=pltpu.CompilerParams(
            collective_id=0, has_side_effects=True, vmem_limit_bytes=60 << 20
        ),
        name="routed_layer",
    )(fwd_in, fwd_ids, fwd_gates, bwd_in, bwd_grad, bwd_ids, bwd_gates, gate_w, up_w, down_w)


def solution(mesh):
    tokens = P("pipe", ("expert", "dp"), None)
    weights = P("pipe", "dp", "expert")
    return jax.shard_map(
        per_device,
        mesh=mesh,
        in_specs=(tokens,) * 7 + (weights,) * 3,
        out_specs=(tokens, tokens, weights),
        check_vma=False,
    )
```

```python
import functools

import jax
import jax.numpy as jnp
from jax import lax
from jax.experimental import pallas as pl
from jax.experimental.pallas import tpu as pltpu
from jax.sharding import PartitionSpec as P

MESH = pl.DeviceIdType.MESH
BF16, F32 = jnp.bfloat16, jnp.float32
X, Z, FW = 0, 1, 2
BACK, OUT = 0, 1
STEP = 256
ROLES = 128
PLACE = {0: 0, 3: 1, 4: 2, 7: 3, 1: 4, 2: 5, 5: 6, 6: 7}

ALL, OWN, REST = 0, 1, 2
SEND_GROUPS = {
    FW: ((0, 7, OWN), (0, 3, REST), (3, 7, REST)),
    X: ((0, 3, ALL), (3, 7, ALL)),
    Z: ((0, 7, ALL),),
}
BACK_GROUPS = {OUT: ((0, 4), (4, 7)), BACK: ((0, 2), (2, 4), (4, 6), (6, 7))}


def kernel(
    sections, holders, cap,
    fwd_in, fwd_ids, fwd_gates, bwd_in, bwd_grad, bwd_ids, bwd_gates, gate_w, up_w, down_w,
    fwd_next, bwd_next, gate_grad,
    raw, wts, packed, recv, sel, slots, gts, pout, pin, acc, hid, part, part_in, ret, fin, grad,
    local_sem, send_sem, recv_sem,
):
    rows = fwd_in.shape[1]
    half, units = gate_w.shape[1], gate_w.shape[2]
    unit = 2 * cap
    quad = 4 * unit
    head = cap - cap % 16
    s, z, q = lax.axis_index("pipe"), lax.axis_index("expert"), lax.axis_index("dp")
    odd = z % 2
    o = 2 * odd - 1

    def at_z(offset):
        return (s, (z + offset * o + holders) % holders, q)

    twin = (s, z, 1 - q)
    mate = at_z(-1)
    section_after, section_before = (s + 1) % sections, (s + sections - 1) % sections
    peers = [twin, mate, at_z(1), at_z(2), at_z(-2), at_z(3)]
    peers += [(t, z, d) for t in (section_after, section_before) for d in (q, 1 - q)]

    roles = []

    def describe(src, dst, device):
        i = len(roles)
        copy = pltpu.make_async_remote_copy(
            src_ref=src, dst_ref=dst, send_sem=send_sem.at[i], recv_sem=recv_sem.at[i],
            device_id=device, device_id_type=MESH,
        )
        roles.append(copy)
        return copy

    def send(src, dst, device):
        copy = describe(src, dst, device)
        copy.start()
        return copy

    def block(j):
        return pl.ds(PLACE[j] * unit, unit)

    def slot_of(j):
        return pl.ds(j * unit, unit)

    def mate_rows(d):
        return pl.ds(pl.multiple_of(d * quad + 2 * unit, 2 * unit), 2 * unit)

    def kept_rows(d):
        return pl.ds(pl.multiple_of(d * quad, 2 * unit), 2 * unit)

    def cols(group):
        return pl.ds(group[0] * STEP, (group[1] - group[0]) * STEP)

    mine = pl.ds(pl.multiple_of(q * rows, rows), rows)
    own_half = pl.ds(pl.multiple_of(q * half, half), half)
    own_rows = pl.ds(pl.multiple_of(q * quad, quad), quad)
    other_rows = pl.ds(pl.multiple_of((1 - q) * quad, quad), quad)
    tokens = {X: bwd_in, Z: bwd_grad, FW: fwd_in}

    loads = {}
    for a in (FW, X, Z):
        loads[a] = pltpu.make_async_copy(
            tokens[a].at[0, :, own_half], raw.at[a, mine, :], local_sem.at[a]
        )
        loads[a].start()
    weight_loads = []
    for i, w in enumerate((gate_w, up_w, down_w)):
        weight_loads.append(pltpu.make_async_copy(w.at[0], wts.at[i], local_sem.at[3 + i]))
        weight_loads[-1].start()

    before = lax.broadcasted_iota(jnp.int32, (rows, rows), 0) < lax.broadcasted_iota(
        jnp.int32, (rows, rows), 1
    )
    pair = (z // 2).astype(F32)
    step_up = (2 - odd).astype(F32)
    step_down = (1 + odd).astype(F32)
    for i, (ids, gates) in enumerate(((bwd_ids, bwd_gates), (fwd_ids, fwd_gates))):
        across = jnp.broadcast_to(ids[0].astype(F32), (rows, rows))
        down = across.T
        same = jnp.where((down == across) & before, 1.0, 0.0)
        rank = jnp.sum(same, axis=0, keepdims=True)
        delta = across[0:1, :] - pair
        delta = jnp.where(delta < 0.0, delta + 4.0, delta)
        place = jnp.where(
            delta == 0.0, 0.0,
            jnp.where(delta == 2.0, 3.0, jnp.where(delta == 1.0, step_up, step_down)),
        )
        side = q.astype(F32)
        within = jnp.where(
            rank < head, side * (unit - head) + rank, head + side * (cap - head) + rank - head
        )
        slot = place * unit + within
        slots[q, pl.ds(8 * i, 8), :] = jnp.broadcast_to(slot, (8, rows))
        slots[q, pl.ds(8 * i + 16, 8), :] = jnp.broadcast_to(gates[0], (8, rows))

    index = lax.broadcasted_iota(jnp.int32, (quad, rows), 0).astype(F32)

    def select(i, b):
        slot = slots[b, 8 * i : 8 * i + 1, :]
        at = pl.ds(pl.multiple_of(b * rows, rows), rows)
        sel[i, :, at] = jnp.where(index == slot, 1.0, 0.0).astype(BF16)

    def piece(kind):
        if kind == ALL:
            return 0, unit
        if kind == OWN:
            return pl.multiple_of(q * (unit - head), 16), head
        return pl.multiple_of((1 - q) * head, 16), unit - head

    def place_rows(a, lo, hi, kind, tokens_at):
        start, size = piece(kind)
        i = 0 if a != FW else 1
        if kind == ALL:
            chosen = sel[i]
        else:
            chosen = jnp.concatenate(
                [sel[i, pl.ds(j * unit + start, size), tokens_at] for j in range(4)], axis=0
            )

        @pl.loop(lo, hi)
        def _(c):
            at = pl.ds(pl.multiple_of(c * STEP, STEP), STEP)
            block_in = raw[a, tokens_at, at]
            if a == Z:
                gate = jnp.concatenate([gts[0, 0][:, 0:1], gts[1, 0][:, 0:1]], axis=0)
                block_in = (gate * block_in.astype(F32)).astype(BF16)
            placed = jnp.dot(chosen, block_in, preferred_element_type=F32).astype(BF16)
            recv[a, pl.ds(start, size), at] = placed[0:size]
            for j in (1, 2, 3):
                packed[a, pl.ds((j - 1) * unit + start, size), at] = placed[j * size : (j + 1) * size]

    loads[FW].wait()
    select(1, q)
    place_rows(FW, 0, half // STEP, OWN, mine)

    barrier = pltpu.get_barrier_semaphore()
    for peer in peers:
        pl.semaphore_signal(barrier, inc=1, device_id=peer, device_id_type=MESH)
    pl.semaphore_wait(barrier, len(peers))

    meta = send(slots.at[q], slots.at[q], twin)
    cross = {}
    for a in (FW, X, Z):
        for group in SEND_GROUPS[a]:
            if group[2] == OWN:
                continue
            width = (group[1] - group[0]) * STEP
            start = pl.multiple_of((1 - q) * half + group[0] * STEP, STEP)
            cross[a, group] = send(
                tokens[a].at[0, :, pl.ds(start, width)], raw.at[a, mine, cols(group)], twin
            )
    direct, passed = {}, {}

    def part_of(ref, a, row, group):
        start, size = piece(group[2])
        return ref.at[a, pl.ds(row + start, size), cols(group)]

    def dispatch(a, n):
        group = SEND_GROUPS[a][n]
        for j, offset in ((2, -2), (0, -1), (3, 3), (1, 1)):
            source = (
                part_of(packed, a, (j - 1) * unit, group) if j else part_of(recv, a, 0, group)
            )
            row = PLACE[j if j else 7] * unit
            direct[a, group, j] = send(source, part_of(recv, a, row, group), at_z(offset))

    def pack(a, n):
        group = SEND_GROUPS[a][n]
        if group[0] == 0 and a != FW:
            loads[a].wait()
        cross[a, group].wait_recv()
        place_rows(a, *group, pl.ds(0, 2 * rows))
        dispatch(a, n)

    def pass_on(a, n):
        group = SEND_GROUPS[a][n]
        for j in (1, 2, 3):
            direct[a, group, j].wait_recv()
            passed[a, group, j] = send(
                part_of(recv, a, PLACE[j] * unit, group),
                part_of(recv, a, PLACE[7 - j] * unit, group),
                mate,
            )

    def arrived(a):
        for group in SEND_GROUPS[a]:
            direct[a, group, 0].wait_recv()
            for j in (1, 2, 3):
                passed[a, group, j].wait_recv()

    dispatch(FW, 0)
    meta.wait_recv()
    select(1, 1 - q)
    for b in range(2):
        for i in range(2):
            gate = slots[b, 8 * i + 16 : 8 * i + 17, :]
            gts[b, i] = jnp.broadcast_to(gate, (rows, rows)).T
        select(0, b)

    def project(a, w, i):
        pout[i] = jnp.dot(recv[a, other_rows, :], wts[w], preferred_element_type=F32).astype(BF16)
        return send(pout.at[i], pin.at[i], twin)

    def project_own(a, w, i):
        acc[i] = jnp.dot(recv[a, own_rows, :], wts[w], preferred_element_type=F32)

    pass_on(FW, 0)
    pack(FW, 1)
    pack(FW, 2)
    pass_on(FW, 1)
    pack(X, 0)
    pack(X, 1)
    pass_on(FW, 2)
    pack(Z, 0)
    pass_on(X, 0)
    arrived(FW)
    for load in weight_loads:
        load.wait()
    sums = {3 + i: project(FW, i, 3 + i) for i in (0, 1)}
    for i in (0, 1):
        project_own(FW, i, i)
    pass_on(X, 1)
    for i in (3, 4):
        sums[i].wait_recv()

    tile = 32

    @pl.loop(0, quad // tile)
    def _(r):
        at = pl.ds(pl.multiple_of(r * tile, tile), tile)
        to = pl.ds(pl.multiple_of(q * quad + r * tile, tile), tile)
        gate = acc[0, at, :] + pin[3, at, :].astype(F32)
        up = acc[1, at, :] + pin[4, at, :].astype(F32)
        hid[2, to, :] = (gate * jax.nn.sigmoid(gate) * up).astype(BF16)

    shared = {2: send(hid.at[2, own_rows, :], hid.at[2, own_rows, :], twin)}

    def expand(r, group, terms, rows_of):
        @pl.loop(group[0], group[1])
        def _(c):
            at = pl.ds(pl.multiple_of(c * STEP, STEP), STEP)
            total = None
            for i, w in terms:
                term = lax.dot_general(
                    hid[i, rows_of, :], wts[w, at, :], (((1,), (1,)), ((), ())),
                    preferred_element_type=F32,
                )
                total = term if total is None else total + term
            part[r, rows_of, at] = total.astype(BF16)

    halves, returned = {}, {}

    def give(r, n, d, step):
        w = cols(BACK_GROUPS[r][n])
        for i, row in enumerate((3 - d, d)):
            source = pl.ds(pl.multiple_of(d * quad + (2 + i) * unit, unit), unit)
            target = pl.ds(pl.multiple_of(row * unit, unit), unit)
            halves[r, n, step, i] = send(part.at[r, source, w], part_in.at[r, target, w], mate)

    def merge(r, n, d, step):
        group = BACK_GROUPS[r][n]
        w = cols(group)
        for i, row in enumerate((3 - d, d)):
            halves[r, n, step, i].wait_recv()
            kept = pl.ds(pl.multiple_of(d * quad + (1 - i) * unit, unit), unit)
            slot = pl.ds(pl.multiple_of(row * unit, unit), unit)

            @pl.loop(group[0], group[1])
            def _(c):
                at = pl.ds(pl.multiple_of(c * STEP, STEP), STEP)
                part[r, kept, at] = (
                    part[r, kept, at].astype(F32) + part_in[r, slot, at].astype(F32)
                ).astype(BF16)

            if i == 0:
                returned[r, n, step] = send(
                    part.at[r, kept, w], ret.at[r, slot, w], at_z(3 - d)
                )
                continue
            if (r, n, 2) not in returned:
                returned[r, n, 2] = describe(
                    part.at[r, block(1), w], ret.at[r, slot_of(1), w], at_z(1)
                )

            @pl.when(d == 1)
            def _():
                returned[r, n, 2].start()

            @pl.when(d == 0)
            def _():
                ret[r, slot_of(0), w] = part[r, block(0), w]

    last = []

    def finish(r, n):
        a, i, section, target = (
            (Z, 0, section_before, bwd_next) if r == BACK else (FW, 1, section_after, fwd_next)
        )
        group = BACK_GROUPS[r][n]
        for j in (0, 1, 2):
            returned[r, n, j].wait_recv()
        for c in range(group[0], group[1], 2):
            at = cols((c, min(c + 2, group[1])))
            picked = lax.dot_general(
                sel[i], ret[r, :, at], (((0,), (0,)), ((), ())), preferred_element_type=F32
            )
            if r == OUT:
                gate = jnp.concatenate([gts[0, 1][:, 0:1], gts[1, 1][:, 0:1]], axis=0)
                picked = gate * picked
            fin[r, :, at] = (raw[a, :, at].astype(F32) + picked).astype(BF16)

        width = (group[1] - group[0]) * STEP
        start = pl.multiple_of(q * half + group[0] * STEP, STEP)
        for device in (1 - q, q):
            from_rows = pl.ds(pl.multiple_of(device * rows, rows), rows)
            last.append(
                send(
                    fin.at[r, from_rows, cols(group)],
                    target.at[0, :, pl.ds(start, width)],
                    (section, z, device),
                )
            )

    arrived(X)
    for i in (0, 1):
        sums[i] = project(X, i, i)
    for i in (0, 1):
        project_own(X, i, i)
    shared[2].wait_recv()
    for n, group in enumerate(BACK_GROUPS[OUT]):
        for d in (q, 1 - q):
            expand(OUT, group, ((2, 2),), mate_rows(d))
        if n == 0:
            for step, d in enumerate((q, 1 - q)):
                give(OUT, 0, d, step)
    pass_on(Z, 0)
    for n in range(1, len(BACK_GROUPS[OUT])):
        for step, d in enumerate((q, 1 - q)):
            give(OUT, n, d, step)
    for group in BACK_GROUPS[OUT]:
        for d in (q, 1 - q):
            expand(OUT, group, ((2, 2),), kept_rows(d))
    for step, d in enumerate((q, 1 - q)):
        merge(OUT, 0, d, step)
    arrived(Z)
    sums[2] = project(Z, 2, 2)
    project_own(Z, 2, 2)
    for i in range(3):
        sums[i].wait_recv()

    @pl.loop(0, quad // tile)
    def _(r):
        at = pl.ds(pl.multiple_of(r * tile, tile), tile)
        to = pl.ds(pl.multiple_of(q * quad + r * tile, tile), tile)
        gate = acc[0, at, :] + pin[0, at, :].astype(F32)
        up = acc[1, at, :] + pin[1, at, :].astype(F32)
        dh = acc[2, at, :] + pin[2, at, :].astype(F32)
        sigma = jax.nn.sigmoid(gate)
        hid[0, to, :] = (dh * up * sigma * (1.0 + gate * (1.0 - sigma))).astype(BF16)
        hid[1, to, :] = (dh * (gate * sigma)).astype(BF16)

    def share(rows_of):
        return [send(hid.at[i, rows_of, :], hid.at[i, rows_of, :], twin) for i in (0, 1)]

    back_terms = ((0, 0), (1, 1))
    back_groups = BACK_GROUPS[BACK]
    first = share(mate_rows(q))
    for n, group in enumerate(back_groups):
        expand(BACK, group, back_terms, mate_rows(q))
        give(BACK, n, q, 0)
    second = share(kept_rows(q))
    for group in back_groups:
        expand(BACK, group, back_terms, kept_rows(q))
    for step, d in enumerate((q, 1 - q)):
        merge(OUT, 1, d, step)
    finish(OUT, 0)
    for copy in first:
        copy.wait_recv()
    for n, group in enumerate(back_groups):
        expand(BACK, group, back_terms, mate_rows(1 - q))
        give(BACK, n, 1 - q, 1)
    for n in range(len(back_groups)):
        merge(BACK, n, q, 0)
    for copy in second:
        copy.wait_recv()
    for group in back_groups:
        expand(BACK, group, back_terms, kept_rows(1 - q))
    @pl.loop(0, half // STEP)
    def _(c):
        at = pl.ds(pl.multiple_of(c * STEP, STEP), STEP)
        grad[at, :] = lax.dot_general(
            recv[X, :, at], hid[0], (((0,), (0,)), ((), ())), preferred_element_type=F32
        ).astype(BF16)

    store = pltpu.make_async_copy(grad, gate_grad.at[0], local_sem.at[6])
    store.start()
    finish(OUT, 1)
    merge(BACK, 0, 1 - q, 1)
    merge(BACK, 1, 1 - q, 1)
    finish(BACK, 0)
    merge(BACK, 2, 1 - q, 1)
    finish(BACK, 1)
    merge(BACK, 3, 1 - q, 1)
    finish(BACK, 2)
    finish(BACK, 3)
    for copy in last:
        copy.wait_recv()
    for copy in roles:
        copy.wait_send()
    store.wait()


def across(column):
    return jnp.transpose(column, (0, 2, 1))


def per_device(
    fwd_in, fwd_ids, fwd_gates, bwd_in, bwd_grad, bwd_ids, bwd_gates, gate_w, up_w, down_w
):
    sections, holders = lax.axis_size("pipe"), lax.axis_size("expert")
    rows, width = fwd_in.shape[1], fwd_in.shape[2]
    half, units = gate_w.shape[1], gate_w.shape[2]
    experts = holders // 2
    cap = rows * 5 // (4 * experts)
    quad = 8 * cap
    hbm = pl.BlockSpec(memory_space=pl.ANY)
    vmem = pl.BlockSpec(memory_space=pltpu.VMEM)
    return pl.pallas_call(
        functools.partial(kernel, sections, holders, cap),
        out_shape=(
            jax.ShapeDtypeStruct(fwd_in.shape, BF16),
            jax.ShapeDtypeStruct(bwd_in.shape, BF16),
            jax.ShapeDtypeStruct(gate_w.shape, BF16),
        ),
        in_specs=[hbm, vmem, vmem, hbm, hbm, vmem, vmem, hbm, hbm, hbm],
        out_specs=(hbm, hbm, hbm),
        scratch_shapes=[
            pltpu.VMEM((3, 2 * rows, half), BF16),
            pltpu.VMEM((3, half, units), BF16),
            pltpu.VMEM((3, 6 * cap, half), BF16),
            pltpu.VMEM((3, 2 * quad, half), BF16),
            pltpu.VMEM((2, quad, 2 * rows), BF16),
            pltpu.VMEM((2, 32, rows), F32),
            pltpu.VMEM((2, 2, rows, rows), F32),
            pltpu.VMEM((5, quad, units), BF16),
            pltpu.VMEM((5, quad, units), BF16),
            pltpu.VMEM((3, quad, units), F32),
            pltpu.VMEM((3, 2 * quad, units), BF16),
            pltpu.VMEM((2, 2 * quad, half), BF16),
            pltpu.VMEM((2, quad, half), BF16),
            pltpu.VMEM((2, quad, half), BF16),
            pltpu.VMEM((2, 2 * rows, half), BF16),
            pltpu.VMEM((half, units), BF16),
            pltpu.SemaphoreType.DMA((7,)),
            pltpu.SemaphoreType.DMA((ROLES,)),
            pltpu.SemaphoreType.DMA((ROLES,)),
        ],
        compiler_params=pltpu.CompilerParams(
            collective_id=0, has_side_effects=True, vmem_limit_bytes=60 << 20
        ),
        name="routed_layer",
    )(
        fwd_in, across(fwd_ids), across(fwd_gates), bwd_in, bwd_grad, across(bwd_ids),
        across(bwd_gates), gate_w, up_w, down_w,
    )


def solution(mesh):
    tokens = P("pipe", ("expert", "dp"), None)
    weights = P("pipe", "dp", "expert")
    return jax.shard_map(
        per_device,
        mesh=mesh,
        in_specs=(tokens,) * 7 + (weights,) * 3,
        out_specs=(tokens, tokens, weights),
        check_vma=False,
    )
```

```python
import functools

import jax
import jax.numpy as jnp
from jax import lax
from jax.experimental import pallas as pl
from jax.experimental.pallas import tpu as pltpu
from jax.sharding import PartitionSpec as P

MESH = pl.DeviceIdType.MESH
BF16, F32 = jnp.bfloat16, jnp.float32
X, Z, FW = 0, 1, 2
BACK, OUT = 0, 1
STEP = 256
ROLES = 128
PLACE = {0: 0, 3: 1, 4: 2, 7: 3, 1: 4, 2: 5, 5: 6, 6: 7}

ALL, OWN, REST = 0, 1, 2
SEND_GROUPS = {
    FW: ((0, 7, OWN), (0, 3, REST), (3, 7, REST)),
    X: ((0, 3, ALL), (3, 7, ALL)),
    Z: ((0, 7, ALL),),
}
BACK_GROUPS = {OUT: ((0, 4), (4, 7)), BACK: ((0, 2), (2, 4), (4, 6), (6, 7))}


def kernel(
    sections, holders, cap,
    fwd_in, fwd_ids, fwd_gates, bwd_in, bwd_grad, bwd_ids, bwd_gates, gate_w, up_w, down_w,
    fwd_next, bwd_next, gate_grad,
    raw, wts, packed, recv, sel, slots, gts, pout, pin, acc, hid, part, part_in, ret, fin, grad,
    local_sem, send_sem, recv_sem,
):
    rows = fwd_in.shape[1]
    half, units = gate_w.shape[1], gate_w.shape[2]
    unit = 2 * cap
    quad = 4 * unit
    head = cap - cap % 16
    s, z, q = lax.axis_index("pipe"), lax.axis_index("expert"), lax.axis_index("dp")
    odd = z % 2
    o = 2 * odd - 1

    def at_z(offset):
        return (s, (z + offset * o + holders) % holders, q)

    twin = (s, z, 1 - q)
    mate = at_z(-1)
    section_after, section_before = (s + 1) % sections, (s + sections - 1) % sections
    peers = [twin, mate, at_z(1), at_z(2), at_z(-2), at_z(3)]
    peers += [(t, z, d) for t in (section_after, section_before) for d in (q, 1 - q)]

    roles = []

    def describe(src, dst, device):
        i = len(roles)
        copy = pltpu.make_async_remote_copy(
            src_ref=src, dst_ref=dst, send_sem=send_sem.at[i], recv_sem=recv_sem.at[i],
            device_id=device, device_id_type=MESH,
        )
        roles.append(copy)
        return copy

    def send(src, dst, device):
        copy = describe(src, dst, device)
        copy.start()
        return copy

    def block(j):
        return pl.ds(PLACE[j] * unit, unit)

    def slot_of(j):
        return pl.ds(j * unit, unit)

    def mate_rows(d):
        return pl.ds(pl.multiple_of(d * quad + 2 * unit, 2 * unit), 2 * unit)

    def kept_rows(d):
        return pl.ds(pl.multiple_of(d * quad, 2 * unit), 2 * unit)

    def cols(group):
        return pl.ds(group[0] * STEP, (group[1] - group[0]) * STEP)

    mine = pl.ds(pl.multiple_of(q * rows, rows), rows)
    own_half = pl.ds(pl.multiple_of(q * half, half), half)
    own_rows = pl.ds(pl.multiple_of(q * quad, quad), quad)
    other_rows = pl.ds(pl.multiple_of((1 - q) * quad, quad), quad)
    tokens = {X: bwd_in, Z: bwd_grad, FW: fwd_in}

    loads = {}
    for a in (FW, X, Z):
        loads[a] = pltpu.make_async_copy(
            tokens[a].at[0, :, own_half], raw.at[a, mine, :], local_sem.at[a]
        )
        loads[a].start()
    weight_loads = []
    for i, w in enumerate((gate_w, up_w, down_w)):
        weight_loads.append(pltpu.make_async_copy(w.at[0], wts.at[i], local_sem.at[3 + i]))
        weight_loads[-1].start()

    before = lax.broadcasted_iota(jnp.int32, (rows, rows), 0) < lax.broadcasted_iota(
        jnp.int32, (rows, rows), 1
    )
    pair = (z // 2).astype(F32)
    step_up = (2 - odd).astype(F32)
    step_down = (1 + odd).astype(F32)
    for i, (ids, gates) in enumerate(((bwd_ids, bwd_gates), (fwd_ids, fwd_gates))):
        across = jnp.broadcast_to(ids[0].astype(F32), (rows, rows))
        down = across.T
        same = jnp.where((down == across) & before, 1.0, 0.0)
        rank = jnp.sum(same, axis=0, keepdims=True)
        delta = across[0:1, :] - pair
        delta = jnp.where(delta < 0.0, delta + 4.0, delta)
        place = jnp.where(
            delta == 0.0, 0.0,
            jnp.where(delta == 2.0, 3.0, jnp.where(delta == 1.0, step_up, step_down)),
        )
        side = q.astype(F32)
        within = jnp.where(
            rank < head, side * (unit - head) + rank, head + side * (cap - head) + rank - head
        )
        slot = place * unit + within
        slots[q, pl.ds(8 * i, 8), :] = jnp.broadcast_to(slot, (8, rows))
        slots[q, pl.ds(8 * i + 16, 8), :] = jnp.broadcast_to(gates[0], (8, rows))

    index = lax.broadcasted_iota(jnp.int32, (quad, rows), 0).astype(F32)

    def select(i, b):
        slot = slots[b, 8 * i : 8 * i + 1, :]
        at = pl.ds(pl.multiple_of(b * rows, rows), rows)
        sel[i, :, at] = jnp.where(index == slot, 1.0, 0.0).astype(BF16)

    def piece(kind):
        if kind == ALL:
            return 0, unit
        if kind == OWN:
            return pl.multiple_of(q * (unit - head), 16), head
        return pl.multiple_of((1 - q) * head, 16), unit - head

    def place_rows(a, lo, hi, kind, tokens_at):
        start, size = piece(kind)
        i = 0 if a != FW else 1
        if kind == ALL:
            chosen = sel[i]
        else:
            chosen = jnp.concatenate(
                [sel[i, pl.ds(j * unit + start, size), tokens_at] for j in range(4)], axis=0
            )

        @pl.loop(lo, hi)
        def _(c):
            at = pl.ds(pl.multiple_of(c * STEP, STEP), STEP)
            block_in = raw[a, tokens_at, at]
            if a == Z:
                gate = jnp.concatenate([gts[0, 0][:, 0:1], gts[1, 0][:, 0:1]], axis=0)
                block_in = (gate * block_in.astype(F32)).astype(BF16)
            placed = jnp.dot(chosen, block_in, preferred_element_type=F32).astype(BF16)
            recv[a, pl.ds(start, size), at] = placed[0:size]
            for j in (1, 2, 3):
                packed[a, pl.ds((j - 1) * unit + start, size), at] = placed[j * size : (j + 1) * size]

    loads[FW].wait()
    select(1, q)
    place_rows(FW, 0, half // STEP, OWN, mine)

    barrier = pltpu.get_barrier_semaphore()
    for peer in peers:
        pl.semaphore_signal(barrier, inc=1, device_id=peer, device_id_type=MESH)
    pl.semaphore_wait(barrier, len(peers))

    meta = send(slots.at[q], slots.at[q], twin)
    cross = {}
    for a in (FW, X, Z):
        for group in SEND_GROUPS[a]:
            if group[2] == OWN:
                continue
            width = (group[1] - group[0]) * STEP
            start = pl.multiple_of((1 - q) * half + group[0] * STEP, STEP)
            cross[a, group] = send(
                tokens[a].at[0, :, pl.ds(start, width)], raw.at[a, mine, cols(group)], twin
            )
    direct, passed = {}, {}

    def part_of(ref, a, row, group):
        start, size = piece(group[2])
        return ref.at[a, pl.ds(row + start, size), cols(group)]

    def dispatch(a, n):
        group = SEND_GROUPS[a][n]
        for j, offset in ((2, -2), (0, -1), (3, 3), (1, 1)):
            source = (
                part_of(packed, a, (j - 1) * unit, group) if j else part_of(recv, a, 0, group)
            )
            row = PLACE[j if j else 7] * unit
            direct[a, group, j] = send(source, part_of(recv, a, row, group), at_z(offset))

    def pack(a, n):
        group = SEND_GROUPS[a][n]
        if group[0] == 0 and a != FW:
            loads[a].wait()
        cross[a, group].wait_recv()
        place_rows(a, *group, pl.ds(0, 2 * rows))
        dispatch(a, n)

    def pass_on(a, n):
        group = SEND_GROUPS[a][n]
        for j in (1, 2, 3):
            direct[a, group, j].wait_recv()
            passed[a, group, j] = send(
                part_of(recv, a, PLACE[j] * unit, group),
                part_of(recv, a, PLACE[7 - j] * unit, group),
                mate,
            )

    def arrived(a):
        for group in SEND_GROUPS[a]:
            direct[a, group, 0].wait_recv()
            for j in (1, 2, 3):
                passed[a, group, j].wait_recv()

    dispatch(FW, 0)
    meta.wait_recv()
    select(1, 1 - q)
    for b in range(2):
        for i in range(2):
            gate = slots[b, 8 * i + 16 : 8 * i + 17, :]
            gts[b, i] = jnp.broadcast_to(gate, (rows, rows)).T
        select(0, b)

    def project(a, w, i):
        pout[i] = jnp.dot(recv[a, other_rows, :], wts[w], preferred_element_type=F32).astype(BF16)
        return send(pout.at[i], pin.at[i], twin)

    def project_own(a, w, i):
        acc[i] = jnp.dot(recv[a, own_rows, :], wts[w], preferred_element_type=F32)

    pass_on(FW, 0)
    pack(FW, 1)
    pack(FW, 2)
    pass_on(FW, 1)
    pack(X, 0)
    pack(X, 1)
    pass_on(FW, 2)
    pack(Z, 0)
    pass_on(X, 0)
    arrived(FW)
    for load in weight_loads:
        load.wait()
    sums = {3 + i: project(FW, i, 3 + i) for i in (0, 1)}
    for i in (0, 1):
        project_own(FW, i, i)
    pass_on(X, 1)
    for i in (3, 4):
        sums[i].wait_recv()

    tile = 32

    @pl.loop(0, quad // tile)
    def _(r):
        at = pl.ds(pl.multiple_of(r * tile, tile), tile)
        to = pl.ds(pl.multiple_of(q * quad + r * tile, tile), tile)
        gate = acc[0, at, :] + pin[3, at, :].astype(F32)
        up = acc[1, at, :] + pin[4, at, :].astype(F32)
        hid[2, to, :] = (gate * jax.nn.sigmoid(gate) * up).astype(BF16)

    shared = {2: send(hid.at[2, own_rows, :], hid.at[2, own_rows, :], twin)}

    def expand(r, group, terms, rows_of):
        @pl.loop(group[0], group[1])
        def _(c):
            at = pl.ds(pl.multiple_of(c * STEP, STEP), STEP)
            total = None
            for i, w in terms:
                term = lax.dot_general(
                    hid[i, rows_of, :], wts[w, at, :], (((1,), (1,)), ((), ())),
                    preferred_element_type=F32,
                )
                total = term if total is None else total + term
            part[r, rows_of, at] = total.astype(BF16)

    halves, returned = {}, {}

    def give(r, n, d, step):
        w = cols(BACK_GROUPS[r][n])
        for i, row in enumerate((3 - d, d)):
            source = pl.ds(pl.multiple_of(d * quad + (2 + i) * unit, unit), unit)
            target = pl.ds(pl.multiple_of(row * unit, unit), unit)
            halves[r, n, step, i] = send(part.at[r, source, w], part_in.at[r, target, w], mate)

    def merge(r, n, d, step):
        group = BACK_GROUPS[r][n]
        w = cols(group)
        for i, row in enumerate((3 - d, d)):
            halves[r, n, step, i].wait_recv()
            kept = pl.ds(pl.multiple_of(d * quad + (1 - i) * unit, unit), unit)
            slot = pl.ds(pl.multiple_of(row * unit, unit), unit)

            @pl.loop(group[0], group[1])
            def _(c):
                at = pl.ds(pl.multiple_of(c * STEP, STEP), STEP)
                part[r, kept, at] = (
                    part[r, kept, at].astype(F32) + part_in[r, slot, at].astype(F32)
                ).astype(BF16)

            if i == 0:
                returned[r, n, step] = send(
                    part.at[r, kept, w], ret.at[r, slot, w], at_z(3 - d)
                )
                continue
            if (r, n, 2) not in returned:
                returned[r, n, 2] = describe(
                    part.at[r, block(1), w], ret.at[r, slot_of(1), w], at_z(1)
                )

            @pl.when(d == 1)
            def _():
                returned[r, n, 2].start()

            @pl.when(d == 0)
            def _():
                ret[r, slot_of(0), w] = part[r, block(0), w]

    last = []

    def finish(r, n):
        a, i, section, target = (
            (Z, 0, section_before, bwd_next) if r == BACK else (FW, 1, section_after, fwd_next)
        )
        group = BACK_GROUPS[r][n]
        for j in (0, 1, 2):
            returned[r, n, j].wait_recv()
        for c in range(group[0], group[1], 2):
            at = cols((c, min(c + 2, group[1])))
            picked = lax.dot_general(
                sel[i], ret[r, :, at], (((0,), (0,)), ((), ())), preferred_element_type=F32
            )
            if r == OUT:
                gate = jnp.concatenate([gts[0, 1][:, 0:1], gts[1, 1][:, 0:1]], axis=0)
                picked = gate * picked
            fin[r, :, at] = (raw[a, :, at].astype(F32) + picked).astype(BF16)

        width = (group[1] - group[0]) * STEP
        start = pl.multiple_of(q * half + group[0] * STEP, STEP)
        for device in (1 - q, q):
            from_rows = pl.ds(pl.multiple_of(device * rows, rows), rows)
            last.append(
                send(
                    fin.at[r, from_rows, cols(group)],
                    target.at[0, :, pl.ds(start, width)],
                    (section, z, device),
                )
            )

    arrived(X)
    for i in (0, 1):
        sums[i] = project(X, i, i)
    for i in (0, 1):
        project_own(X, i, i)
    shared[2].wait_recv()
    for n, group in enumerate(BACK_GROUPS[OUT]):
        for d in (q, 1 - q):
            expand(OUT, group, ((2, 2),), mate_rows(d))
        if n == 0:
            for step, d in enumerate((q, 1 - q)):
                give(OUT, 0, d, step)
    pass_on(Z, 0)
    for n in range(1, len(BACK_GROUPS[OUT])):
        for step, d in enumerate((q, 1 - q)):
            give(OUT, n, d, step)
    for group in BACK_GROUPS[OUT]:
        for d in (q, 1 - q):
            expand(OUT, group, ((2, 2),), kept_rows(d))
    for step, d in enumerate((q, 1 - q)):
        merge(OUT, 0, d, step)
    arrived(Z)
    sums[2] = project(Z, 2, 2)
    project_own(Z, 2, 2)
    for i in range(3):
        sums[i].wait_recv()

    @pl.loop(0, quad // tile)
    def _(r):
        at = pl.ds(pl.multiple_of(r * tile, tile), tile)
        to = pl.ds(pl.multiple_of(q * quad + r * tile, tile), tile)
        gate = acc[0, at, :] + pin[0, at, :].astype(F32)
        up = acc[1, at, :] + pin[1, at, :].astype(F32)
        dh = acc[2, at, :] + pin[2, at, :].astype(F32)
        sigma = jax.nn.sigmoid(gate)
        hid[0, to, :] = (dh * up * sigma * (1.0 + gate * (1.0 - sigma))).astype(BF16)
        hid[1, to, :] = (dh * (gate * sigma)).astype(BF16)

    def share(rows_of):
        return [send(hid.at[i, rows_of, :], hid.at[i, rows_of, :], twin) for i in (0, 1)]

    back_terms = ((0, 0), (1, 1))
    back_groups = BACK_GROUPS[BACK]
    first = share(mate_rows(q))
    for n, group in enumerate(back_groups):
        expand(BACK, group, back_terms, mate_rows(q))
        give(BACK, n, q, 0)
    second = share(kept_rows(q))
    for group in back_groups:
        expand(BACK, group, back_terms, kept_rows(q))
    for step, d in enumerate((q, 1 - q)):
        merge(OUT, 1, d, step)
    finish(OUT, 0)
    for copy in first:
        copy.wait_recv()
    for n, group in enumerate(back_groups):
        expand(BACK, group, back_terms, mate_rows(1 - q))
        give(BACK, n, 1 - q, 1)
    for n in range(len(back_groups)):
        merge(BACK, n, q, 0)
    for copy in second:
        copy.wait_recv()
    for group in back_groups:
        expand(BACK, group, back_terms, kept_rows(1 - q))
    @pl.loop(0, half // STEP)
    def _(c):
        at = pl.ds(pl.multiple_of(c * STEP, STEP), STEP)
        grad[at, :] = lax.dot_general(
            recv[X, :, at], hid[0], (((0,), (0,)), ((), ())), preferred_element_type=F32
        ).astype(BF16)

    store = pltpu.make_async_copy(grad, gate_grad.at[0], local_sem.at[6])
    store.start()
    finish(OUT, 1)
    merge(BACK, 0, 1 - q, 1)
    merge(BACK, 1, 1 - q, 1)
    finish(BACK, 0)
    merge(BACK, 2, 1 - q, 1)
    finish(BACK, 1)
    merge(BACK, 3, 1 - q, 1)
    finish(BACK, 2)
    finish(BACK, 3)
    for copy in last:
        copy.wait_recv()
    for copy in roles:
        copy.wait_send()
    store.wait()


def hand_over(*refs):
    copies = []
    for i in range(3):
        rows = refs[i].shape[1] // 4
        for j in range(4):
            part = pl.ds(j * rows, rows)
            copies.append(
                pltpu.make_async_copy(
                    refs[i].at[0, part], refs[3 + i].at[0, part], refs[6].at[4 * i + j]
                )
            )
            copies[-1].start()
    for copy in copies:
        copy.wait()


def across(column):
    return jnp.transpose(column, (0, 2, 1))


def per_device(
    fwd_in, fwd_ids, fwd_gates, bwd_in, bwd_grad, bwd_ids, bwd_gates, gate_w, up_w, down_w
):
    sections, holders = lax.axis_size("pipe"), lax.axis_size("expert")
    rows, width = fwd_in.shape[1], fwd_in.shape[2]
    half, units = gate_w.shape[1], gate_w.shape[2]
    experts = holders // 2
    cap = rows * 5 // (4 * experts)
    quad = 8 * cap
    hbm = pl.BlockSpec(memory_space=pl.ANY)
    vmem = pl.BlockSpec(memory_space=pltpu.VMEM)
    results = pl.pallas_call(
        functools.partial(kernel, sections, holders, cap),
        out_shape=(
            jax.ShapeDtypeStruct(fwd_in.shape, BF16),
            jax.ShapeDtypeStruct(bwd_in.shape, BF16),
            jax.ShapeDtypeStruct(gate_w.shape, BF16),
        ),
        in_specs=[hbm, vmem, vmem, hbm, hbm, vmem, vmem, hbm, hbm, hbm],
        out_specs=(hbm, hbm, hbm),
        scratch_shapes=[
            pltpu.VMEM((3, 2 * rows, half), BF16),
            pltpu.VMEM((3, half, units), BF16),
            pltpu.VMEM((3, 6 * cap, half), BF16),
            pltpu.VMEM((3, 2 * quad, half), BF16),
            pltpu.VMEM((2, quad, 2 * rows), BF16),
            pltpu.VMEM((2, 32, rows), F32),
            pltpu.VMEM((2, 2, rows, rows), F32),
            pltpu.VMEM((5, quad, units), BF16),
            pltpu.VMEM((5, quad, units), BF16),
            pltpu.VMEM((3, quad, units), F32),
            pltpu.VMEM((3, 2 * quad, units), BF16),
            pltpu.VMEM((2, 2 * quad, half), BF16),
            pltpu.VMEM((2, quad, half), BF16),
            pltpu.VMEM((2, quad, half), BF16),
            pltpu.VMEM((2, 2 * rows, half), BF16),
            pltpu.VMEM((half, units), BF16),
            pltpu.SemaphoreType.DMA((7,)),
            pltpu.SemaphoreType.DMA((ROLES,)),
            pltpu.SemaphoreType.DMA((ROLES,)),
        ],
        compiler_params=pltpu.CompilerParams(
            collective_id=0, has_side_effects=True, vmem_limit_bytes=60 << 20
        ),
        name="routed_layer",
    )(
        fwd_in, across(fwd_ids), across(fwd_gates), bwd_in, bwd_grad, across(bwd_ids),
        across(bwd_gates), gate_w, up_w, down_w,
    )
    return pl.pallas_call(
        hand_over,
        out_shape=tuple(jax.ShapeDtypeStruct(r.shape, r.dtype) for r in results),
        in_specs=[hbm] * 3,
        out_specs=(hbm,) * 3,
        scratch_shapes=[pltpu.SemaphoreType.DMA((12,))],
        name="hand_over",
    )(*results)


def solution(mesh):
    tokens = P("pipe", ("expert", "dp"), None)
    weights = P("pipe", "dp", "expert")
    return jax.shard_map(
        per_device,
        mesh=mesh,
        in_specs=(tokens,) * 7 + (weights,) * 3,
        out_specs=(tokens, tokens, weights),
        check_vma=False,
    )
```
